32 devices in a mesh: row: 8 (over z, y), col: 4 (over x, core).
Axes of the slice: x: 2, y: 2, z: 4, core: 2. Of those that a mesh axis runs over, the one named last changes fastest.
Arguments:
- features: bfloat16 [4096, 256], P(('col', 'row')), may hold values from -6 to 6
- tile_values: bfloat16 [8, 4, 32, 128, 128], P('row', 'col'), may hold values from -0.125 to 0.125
- tile_rows: int32 [8, 4, 32], P('row', 'col'), may hold values from 0 to 3
- tile_cols: int32 [8, 4, 32], P('row', 'col'), may hold values from 0 to 7
- live_slots: int32 [8, 4], P('row', 'col'), may hold values from 4 to 32, as said below
- weight: bfloat16 [256, 256], replicated, may hold values from -0.375 to 0.375
- bias_vector: float32 [256], replicated, may hold values from -3 to 3
- cotangent: bfloat16 [4096, 256], P(('row', 'col')), may hold values from -6 to 6
Outputs:
- output: bfloat16 [4096, 256], P(('row', 'col'))
- grad_features: float32 [4096, 256], P(('col', 'row'))
- grad_weight: float32 [256, 256], replicated
The draws below stay inside these ranges and needn't reach their ends.
Inputs may be any that keep to these rules, and one draw needn't show every extreme that they name: `live_slots`: some block uses all 32 slots.
All inputs are finite; a program needn't handle non-finite values.
Results may differ from the reference program's by a relative error of at most 0.0058.
Values may be sent and summed in bfloat16 or wider, within the bound.
A program may use at most 64 MiB of HBM per device.

```python
import jax
import jax.numpy as jnp
from jax import lax

IN_FEAT = 256
OUT_FEAT = 256
TILE = 128
SLOTS = 32
TILE_ROWS = 4
TILE_COLS = 8
NODES = 4096
N_ROW = 8
N_COL = 4


def draw_live_slots(key, part):
    key = jax.random.fold_in(key, 3)
    first_key, second_key = jax.random.split(key)
    shifts = jax.random.randint(first_key, (N_ROW * N_COL,), 0, 4)
    counts = SLOTS // 2 ** shifts
    chosen = jax.random.randint(second_key, (), 0, N_ROW * N_COL)
    counts = counts.at[chosen].set(SLOTS)
    return counts.reshape(N_ROW, N_COL).astype(jnp.int32)


def set_ends(result, own_key, smallest, high):
    spot = [jax.random.randint(jax.random.fold_in(own_key, axis), (), 0, length) for axis, length in enumerate(result.shape)]
    longest = result.shape.index(max(result.shape))
    neighbour = spot[:longest] + [(spot[longest] + 1) % result.shape[longest]] + spot[longest + 1:]
    return result.at[tuple(spot)].set(smallest).at[tuple(neighbour)].set(high)


def block_scale(rng, shape, cuts, smallest, top_value):
    def one(axis_at, blocks):
        heights = jax.random.uniform(jax.random.fold_in(jax.random.fold_in(rng, 6), axis_at), (blocks,), jnp.float32, smallest / len(cuts), top_value / len(cuts))
        return jnp.repeat(jnp.exp(heights), shape[axis_at] // blocks).reshape((-1,) + (1,) * (len(shape) - axis_at - 1))

    level = one(*cuts[0])
    for cut in cuts[1:]:
        level = level * one(*cut)
    return level


def gaussian(own_key, dims, spread, most, cuts=(), kind=jnp.bfloat16):
    result = spread * jax.random.normal(own_key, dims, jnp.float32)
    if cuts:
        result = result * block_scale(own_key, dims, cuts, -0.22, 0.18)
    return jnp.clip(result, -most, most).astype(kind)


def setup_inputs(seed: int = 0) -> dict:
    keys = jax.random.split(jax.random.key(seed), 9)
    return {
        "features": gaussian(keys[0], (NODES, IN_FEAT), 1.0, 6.0, ((0, 32),)),
        "tile_values": gaussian(keys[1], (N_ROW, N_COL, SLOTS, TILE, TILE), (TILE * SLOTS * N_COL // (2 * TILE_ROWS)) ** -0.5, 0.125, ((0, 8), (1, 4))),
        "tile_rows": set_ends(jax.random.randint(keys[2], (N_ROW, N_COL, SLOTS), 0, TILE_ROWS), jax.random.fold_in(keys[2], 1), 0, TILE_ROWS - 1).astype(jnp.int32),
        "tile_cols": set_ends(jax.random.randint(keys[3], (N_ROW, N_COL, SLOTS), 0, TILE_COLS), jax.random.fold_in(keys[3], 1), 0, TILE_COLS - 1).astype(jnp.int32),
        "live_slots": draw_live_slots(jax.random.fold_in(keys[8], 71), 0),
        "weight": gaussian(keys[5], (IN_FEAT, OUT_FEAT), IN_FEAT ** -0.5, 0.375),
        "bias_vector": gaussian(keys[6], (OUT_FEAT,), 0.5, 3.0, (), jnp.float32),
        "cotangent": gaussian(keys[7], (NODES, OUT_FEAT), 1.0, 6.0, ((0, 32),)),
    }


def reference(features, tile_values, tile_rows, tile_cols, live_slots, weight, bias_vector, cotangent):
    column_blocks = features.reshape(N_COL, TILE_COLS, TILE, IN_FEAT)
    slot_index = jnp.arange(SLOTS).astype(jnp.int32)
    col_index = jnp.arange(N_COL).astype(jnp.int32)

    def forward_row(row_index):
        tile_block = tile_values[row_index]
        row_ids = tile_rows[row_index]
        col_ids = tile_cols[row_index]
        live_count = live_slots[row_index]
        picked = column_blocks[col_index[:, None], col_ids]
        products = jnp.einsum("jsab,jsbf->jsaf", tile_block.astype(jnp.float32), picked.astype(jnp.float32))
        one_hot = ((row_ids[..., None] == jnp.arange(TILE_ROWS).astype(jnp.int32)) & (slot_index[None, :, None] < live_count[:, None, None])).astype(jnp.float32)
        return jnp.einsum("jsr,jsaf->raf", one_hot, products, precision=lax.Precision.HIGHEST)

    partial_value = lax.map(forward_row, jnp.arange(N_ROW).astype(jnp.int32))
    aggregate = partial_value.reshape(NODES, IN_FEAT).astype(jnp.bfloat16)
    preact = jnp.dot(aggregate, weight, preferred_element_type=jnp.float32) + bias_vector
    sigmoid_z = jax.nn.sigmoid(preact)
    output = (preact * sigmoid_z).astype(jnp.bfloat16)
    grad_pre = (cotangent.astype(jnp.float32) * sigmoid_z * (1.0 + preact * (1.0 - sigmoid_z))).astype(jnp.bfloat16)
    grad_aggregate = jnp.dot(grad_pre, weight.T, preferred_element_type=jnp.float32).astype(jnp.bfloat16)
    grad_weight = jnp.dot(aggregate.T, grad_pre, preferred_element_type=jnp.float32)
    row_blocks = grad_aggregate.reshape(N_ROW, TILE_ROWS, TILE, IN_FEAT)

    def backward_row(running, row_index):
        tile_block = tile_values[row_index]
        row_ids = tile_rows[row_index]
        col_ids = tile_cols[row_index]
        live_count = live_slots[row_index]
        picked = row_blocks[row_index][row_ids]
        products = jnp.einsum("jsab,jsaf->jsbf", tile_block.astype(jnp.float32), picked.astype(jnp.float32))
        one_hot = ((col_ids[..., None] == jnp.arange(TILE_COLS).astype(jnp.int32)) & (slot_index[None, :, None] < live_count[:, None, None])).astype(jnp.float32)
        return running + jnp.einsum("jsc,jsbf->jcbf", one_hot, products, precision=lax.Precision.HIGHEST), None

    start = jnp.zeros((N_COL, TILE_COLS, TILE, IN_FEAT), jnp.float32)
    total, unused = lax.scan(backward_row, start, jnp.arange(N_ROW).astype(jnp.int32))
    grad_features = total.reshape(NODES, IN_FEAT)
    return output, grad_features, grad_weight
```

```python
import functools

import jax
import jax.numpy as jnp
from jax import lax
from jax.experimental import pallas as pl
from jax.experimental.pallas import tpu as pltpu
from jax.sharding import PartitionSpec as P

F32 = jnp.float32
BF16 = jnp.bfloat16
GROUP = 16


def loop(count, body):
    if count <= 8:
        for step in range(count):
            body(step)
    else:
        lax.fori_loop(0, count, lambda step, carry: (body(step), carry)[1], 0)


def dot(a, b, dims=((1,), (0,))):
    return lax.dot_general(a, b, (dims, ((), ())), preferred_element_type=F32)


def kernel(
    n_row, n_col, fused_weight, pre_transpose,
    feat, tiles_hbm, row_ids, col_ids, live, weight, bias, cot,
    out, grad_feat, grad_w,
    tiles, adj, adj_t, gathered, acc, part_send, part_recv, grads, back_send, back_recv,
    w_local, w_col, w_piece, w_row, w_final, w_all,
    tile_sem, x_send, x_recv, p_send, p_recv, g_send, g_recv, b_send, b_recv,
    w1_send, w1_recv, w2_send, w2_recv, w3_send, w3_recv, w4_send, w4_recv,
):
    i = lax.axis_index("row")
    j = lax.axis_index("col")
    size = feat.shape[0]
    width = feat.shape[1]
    slots = tiles.shape[0]

    def row_peer(k):
        return lax.rem(i + k, n_row)

    def col_peer(k):
        return lax.rem(j + k, n_col)

    def send(src, dst, send_sem, recv_sem, axis, peer):
        return pltpu.make_async_remote_copy(
            src_ref=src, dst_ref=dst, send_sem=send_sem, recv_sem=recv_sem,
            device_id={axis: peer}, device_id_type=pl.DeviceIdType.MESH,
        )

    tile_copy = pltpu.make_async_copy(tiles_hbm.at[0, 0], tiles, tile_sem)
    tile_copy.start()

    barrier = pltpu.get_barrier_semaphore()

    def greet_row(k):
        pl.semaphore_signal(
            barrier, inc=1, device_id={"row": row_peer(k + 1)}, device_id_type=pl.DeviceIdType.MESH
        )

    def greet_col(k):
        pl.semaphore_signal(
            barrier, inc=1, device_id={"col": col_peer(k + 1)}, device_id_type=pl.DeviceIdType.MESH
        )

    loop(n_row - 1, greet_row)
    loop(n_col - 1, greet_col)
    pl.semaphore_wait(barrier, n_row + n_col - 2)

    def x_copy(to, sender):
        return send(feat, gathered.at[sender], x_send.at[to], x_recv.at[sender], "row", to)

    loop(n_row - 1, lambda k: x_copy(row_peer(k + 1), i).start())

    tile_copy.wait()
    depth = slots * GROUP
    together = n_row if n_row * n_col <= 64 else 1
    cells = together * n_col
    spread_in = (
        lax.broadcasted_iota(jnp.int32, (slots, depth), 1) // GROUP
        == lax.broadcasted_iota(jnp.int32, (slots, depth), 0)
    ).astype(BF16)
    spread_out = (
        lax.broadcasted_iota(jnp.int32, (cells * GROUP, cells), 0) // GROUP
        == lax.broadcasted_iota(jnp.int32, (cells * GROUP, cells), 1)
    ).astype(BF16)
    same_line = (
        lax.broadcasted_iota(jnp.int32, (cells * GROUP, depth), 0) % GROUP
        == lax.broadcasted_iota(jnp.int32, (cells * GROUP, depth), 1) % GROUP
    )
    cell_of = col_ids[0] * n_col + row_ids[0]
    cell_of = jnp.where(
        lax.broadcasted_iota(jnp.int32, (1, slots), 1) < live[...], cell_of, -1
    )

    def densify(step):
        cell_index = lax.broadcasted_iota(jnp.int32, (cells, slots), 0) + step * cells
        chosen = (cell_index == cell_of).astype(BF16)
        picked = dot(spread_out, dot(chosen, spread_in).astype(BF16))
        picked = jnp.where(same_line, picked, 0.0).astype(BF16)
        for pair in range(size // GROUP // 2):
            lines = [
                tiles[:, (2 * pair + h) * GROUP:(2 * pair + h + 1) * GROUP, :].reshape(depth, size)
                for h in range(2)
            ]
            block = dot(picked, jnp.concatenate(lines, axis=1)).astype(BF16)
            for c in range(together):
                for r in range(n_col):
                    at = (c * n_col + r) * GROUP
                    for h in range(2):
                        line = r * size + (2 * pair + h) * GROUP
                        adj[step * together + c, line:line + GROUP, :] = (
                            block[at:at + GROUP, h * size:(h + 1) * size]
                        )
        if pre_transpose:
            for c in range(together):
                adj_t[step * together + c] = adj[step * together + c].T

    loop(n_row // together, densify)

    rows = n_col * size
    chunk = min(rows, 512)

    def add_block(b, block, first):
        def one(step):
            at = pl.ds(step * chunk, chunk)
            product = dot(adj[b, at, :], block)
            if first:
                acc[at, :] = product
            else:
                acc[at, :] += product
        loop(rows // chunk, one)

    add_block(i, feat[...], True)

    def take_features(k):
        sender = lax.rem(i + n_row - 1 - k, n_row)
        x_copy(sender, sender).wait_recv()
        add_block(sender, gathered[sender], False)

    loop(n_row - 1, take_features)

    def p_copy(to, sender):
        return send(
            part_send.at[to], part_recv.at[sender], p_send.at[to], p_recv.at[sender], "col", to
        )

    def send_partial(k):
        to = col_peer(k + 1)
        part_send[to] = acc[pl.ds(pl.multiple_of(to * size, size), size), :].astype(BF16)
        p_copy(to, j).start()

    loop(n_col - 1, send_partial)
    acc_own = pl.ds(pl.multiple_of(j * size, size), size)

    def take_partial(k):
        sender = lax.rem(j + n_col - 1 - k, n_col)
        p_copy(sender, sender).wait_recv()
        acc[acc_own, :] += part_recv[sender].astype(F32)

    loop(n_col - 1, take_partial)

    aggregate = acc[acc_own, :].astype(BF16)
    preact = dot(aggregate, weight[...]) + bias[...]
    sig = jax.nn.sigmoid(preact)
    grad_pre = (cot[...].astype(F32) * sig * (1.0 + preact * (1.0 - sig))).astype(BF16)
    grads[j] = dot(grad_pre, weight[...], ((1,), (1,))).astype(BF16)

    def g_copy(to, sender):
        return send(grads.at[j], grads.at[sender], g_send.at[to], g_recv.at[sender], "col", to)

    loop(n_col - 1, lambda k: g_copy(col_peer(k + 1), j).start())

    out[...] = (preact * sig).astype(BF16)
    local_weight = dot(aggregate, grad_pre, ((0,), (0,)))

    if fused_weight:
        piece = width // n_col
        strip = piece // n_row
        w_local[...] = local_weight.reshape(n_col, piece, width).astype(BF16)

        def w1_copy(to, sender):
            return send(
                w_local.at[to], w_col.at[sender], w1_send.at[to], w1_recv.at[sender], "col", to
            )

        loop(n_col - 1, lambda k: w1_copy(col_peer(k + 1), j).start())
    else:
        grad_w[...] = local_weight

    def take_grad(k):
        sender = lax.rem(j + n_col - 1 - k, n_col)
        g_copy(sender, sender).wait_recv()

    loop(n_col - 1, take_grad)

    def back(b):
        if pre_transpose:
            return dot(adj_t[b], grads[...].reshape(rows, width))
        return dot(adj[b], grads[...].reshape(rows, width), ((0,), (0,)))

    def b_copy(to, sender):
        return send(
            back_send.at[to], back_recv.at[sender], b_send.at[to], b_recv.at[sender], "row", to
        )

    def send_back(k):
        to = row_peer(k + 1)
        back_send[to] = back(to).astype(BF16)
        b_copy(to, i).start()

    loop(n_row - 1, send_back)
    grad_feat[...] = back(i)

    if fused_weight:
        total = w_local[j].astype(F32)
        for k in range(n_col - 1):
            sender = lax.rem(j + n_col - 1 - k, n_col)
            w1_copy(sender, sender).wait_recv()
            total += w_col[sender].astype(F32)
        w_piece[...] = total.reshape(n_row, strip, width)

        def w2_copy(to, sender):
            return send(
                w_piece.at[to], w_row.at[sender], w2_send.at[to], w2_recv.at[sender], "row", to
            )

        loop(n_row - 1, lambda k: w2_copy(row_peer(k + 1), i).start())
        total = w_piece[i]
        for k in range(n_row - 1):
            sender = lax.rem(i + n_row - 1 - k, n_row)
            w2_copy(sender, sender).wait_recv()
            total += w_row[sender]
        w_final[i] = total

        def w3_copy(to, sender):
            return send(
                w_final.at[i], w_final.at[sender], w3_send.at[to], w3_recv.at[sender], "row", to
            )

        loop(n_row - 1, lambda k: w3_copy(row_peer(k + 1), i).start())
        for k in range(n_row - 1):
            sender = lax.rem(i + n_row - 1 - k, n_row)
            w3_copy(sender, sender).wait_recv()

        def w4_copy(to, sender):
            return send(
                w_final, w_all.at[sender], w4_send.at[to], w4_recv.at[sender], "col", to
            )

        loop(n_col - 1, lambda k: w4_copy(col_peer(k + 1), j).start())
        grad_w[j] = w_final[...].reshape(piece, width)

    def take_back(k):
        sender = lax.rem(i + n_row - 1 - k, n_row)
        b_copy(sender, sender).wait_recv()
        grad_feat[...] += back_recv[sender].astype(F32)

    loop(n_row - 1, take_back)

    if fused_weight:
        for k in range(n_col - 1):
            sender = lax.rem(j + n_col - 1 - k, n_col)
            w4_copy(sender, sender).wait_recv()
            grad_w[sender] = w_all[sender].reshape(piece, width)

    def row_sent(k):
        to = row_peer(k + 1)
        x_copy(to, i).wait_send()
        b_copy(to, i).wait_send()
        if fused_weight:
            w2_copy(to, i).wait_send()
            w3_copy(to, i).wait_send()

    def col_sent(k):
        to = col_peer(k + 1)
        p_copy(to, j).wait_send()
        g_copy(to, j).wait_send()
        if fused_weight:
            w1_copy(to, j).wait_send()
            w4_copy(to, j).wait_send()

    loop(n_row - 1, row_sent)
    loop(n_col - 1, col_sent)


def shards(n_row, n_col, features, tile_values, tile_rows, tile_cols, live_slots, weight, bias, cotangent):
    size, width = features.shape
    slots = tile_values.shape[2]
    out_width = weight.shape[1]
    rows = n_col * size
    fused_weight = width % (n_col * n_row * 8) == 0
    pre_transpose = n_row * n_col <= 64
    piece = width // n_col if fused_weight else 16
    strip = piece // n_row if fused_weight else 8
    w_shape = (n_col, piece, out_width) if fused_weight else (width, out_width)
    vmem = pl.BlockSpec(memory_space=pltpu.VMEM)
    row_dma = pltpu.SemaphoreType.DMA((n_row,))
    col_dma = pltpu.SemaphoreType.DMA((n_col,))
    out, grad_features, grad_weight = pl.pallas_call(
        functools.partial(kernel, n_row, n_col, fused_weight, pre_transpose),
        out_shape=(
            jax.ShapeDtypeStruct((size, out_width), BF16),
            jax.ShapeDtypeStruct((size, width), F32),
            jax.ShapeDtypeStruct(w_shape, F32),
        ),
        in_specs=[vmem, pl.BlockSpec(memory_space=pl.ANY)] + [vmem] * 6,
        out_specs=(vmem, vmem, vmem),
        scratch_shapes=[
            pltpu.VMEM((slots, size, size), BF16),
            pltpu.VMEM((n_row, rows, size), BF16),
            pltpu.VMEM((n_row, size, rows) if pre_transpose else (1, 16, 128), BF16),
            pltpu.VMEM((n_row, size, width), BF16),
            pltpu.VMEM((rows, width), F32),
            pltpu.VMEM((n_col, size, width), BF16),
            pltpu.VMEM((n_col, size, width), BF16),
            pltpu.VMEM((n_col, size, width), BF16),
            pltpu.VMEM((n_row, size, width), BF16),
            pltpu.VMEM((n_row, size, width), BF16),
            pltpu.VMEM((n_col, piece, out_width), BF16),
            pltpu.VMEM((n_col, piece, out_width), BF16),
            pltpu.VMEM((n_row, strip, out_width), F32),
            pltpu.VMEM((n_row, strip, out_width), F32),
            pltpu.VMEM((n_row, strip, out_width), F32),
            pltpu.VMEM((n_col, n_row, strip, out_width), F32),
            pltpu.SemaphoreType.DMA,
            row_dma, row_dma, col_dma, col_dma, col_dma, col_dma, row_dma, row_dma,
            col_dma, col_dma, row_dma, row_dma, row_dma, row_dma, col_dma, col_dma,
        ],
        compiler_params=pltpu.CompilerParams(
            collective_id=0, has_side_effects=True, vmem_limit_bytes=56 * 1024 * 1024
        ),
    )(
        features, tile_values, tile_rows, tile_cols, live_slots,
        weight, bias.reshape(1, out_width), cotangent,
    )
    if fused_weight:
        return out, grad_features, grad_weight.reshape(width, out_width)
    return out, grad_features, lax.psum(grad_weight, ("row", "col"))


def solution(mesh):
    return jax.shard_map(
        functools.partial(shards, mesh.shape["row"], mesh.shape["col"]),
        mesh=mesh,
        in_specs=(
            P(("col", "row"), None),
            P("row", "col", None, None, None),
            P("row", "col", None),
            P("row", "col", None),
            P("row", "col"),
            P(),
            P(),
            P(("row", "col"), None),
        ),
        out_specs=(P(("row", "col"), None), P(("col", "row"), None), P()),
        check_vma=False,
    )
```

```python
import functools

import jax
import jax.numpy as jnp
from jax import lax
from jax.experimental import pallas as pl
from jax.experimental.pallas import tpu as pltpu
from jax.sharding import PartitionSpec as P

F32 = jnp.float32
BF16 = jnp.bfloat16
GROUP = 16


def loop(count, body):
    if count <= 8:
        for step in range(count):
            body(step)
    else:
        lax.fori_loop(0, count, lambda step, carry: (body(step), carry)[1], 0)


def dot(a, b, dims=((1,), (0,))):
    return lax.dot_general(a, b, (dims, ((), ())), preferred_element_type=F32)


def kernel(
    n_row, n_col, outer, pre_transpose,
    feat, tiles_hbm, row_ids, col_ids, live, weight, bias, cot,
    out, grad_feat, grad_w,
    tiles, adj, adj_t, gathered, acc, part_send, part_recv, grads,
    y_out, y_in, keep, z_out, z_in, w_out, w_in, w_sum, w_cols, w_all,
    tile_sem, xz_send, xy_send, x_recv, p_send, p_recv, g_send, g_recv,
    by_send, by_recv, bz_send, bz_recv,
    w1_send, w1_recv, w2_send, w2_recv, w3z_send, w3y_send, w3_recv,
):
    i = lax.axis_index("row")
    j = lax.axis_index("col")
    inner = n_row // outer
    z = i // inner
    y = i % inner
    size = feat.shape[0]
    slots = tiles.shape[0]

    def row_peer(k):
        return lax.rem(i + k, n_row)

    def col_peer(k):
        return lax.rem(j + k, n_col)

    def y_peer(k):
        return lax.rem(y + k, inner)

    if outer == 4:
        near, mid, far = z + 1 - 2 * (z % 2), (z + 2) % 4, 3 - z
        z_near_first, z_far_first = (near, mid, far), (mid, far, near)
    else:
        z_near_first = z_far_first = tuple((z + k) % outer for k in range(1, outer))

    def send(src, dst, send_sem, recv_sem, axis, peer):
        return pltpu.make_async_remote_copy(
            src_ref=src, dst_ref=dst, send_sem=send_sem, recv_sem=recv_sem,
            device_id={axis: peer}, device_id_type=pl.DeviceIdType.MESH,
        )

    tile_copy = pltpu.make_async_copy(tiles_hbm.at[0, 0], tiles, tile_sem)
    tile_copy.start()

    barrier = pltpu.get_barrier_semaphore()

    def greet_row(k):
        pl.semaphore_signal(
            barrier, inc=1, device_id={"row": row_peer(k + 1)}, device_id_type=pl.DeviceIdType.MESH
        )

    def greet_col(k):
        pl.semaphore_signal(
            barrier, inc=1, device_id={"col": col_peer(k + 1)}, device_id_type=pl.DeviceIdType.MESH
        )

    loop(n_row - 1, greet_row)
    loop(n_col - 1, greet_col)
    gathered[i] = feat[...]
    pl.semaphore_wait(barrier, n_row + n_col - 2)

    def along_z(buf, z_sem, recv_sem, to, block):
        return send(
            buf.at[block], buf.at[block], z_sem.at[to], recv_sem.at[block], "row", to * inner + y
        )

    def along_y(buf, y_sem, recv_sem, block_z, to, block):
        return send(
            buf.at[block], buf.at[block], y_sem.at[block_z * inner + to], recv_sem.at[block],
            "row", z * inner + to,
        )

    def gather_start(buf, z_sem, y_sem, recv_sem):
        for to in z_far_first:
            along_z(buf, z_sem, recv_sem, to, i).start()
        loop(inner - 1, lambda k: along_y(buf, y_sem, recv_sem, z, y_peer(k + 1), i).start())

    def gather_pass(buf, z_sem, y_sem, recv_sem, block_z):
        block = block_z * inner + y
        along_z(buf, z_sem, recv_sem, block_z, block).wait_recv()
        loop(
            inner - 1,
            lambda k: along_y(buf, y_sem, recv_sem, block_z, y_peer(k + 1), block).start(),
        )
        return block

    def gather_take(buf, y_sem, recv_sem, block_z, from_y):
        block = block_z * inner + from_y
        along_y(buf, y_sem, recv_sem, block_z, from_y, block).wait_recv()
        return block

    def gather_sent(buf, z_sem, y_sem, recv_sem):
        for to in z_near_first:
            along_z(buf, z_sem, recv_sem, to, i).wait_send()
        for block_z in (z,) + z_near_first:
            loop(
                inner - 1,
                lambda k: along_y(
                    buf, y_sem, recv_sem, block_z, y_peer(k + 1), block_z * inner + y
                ).wait_send(),
            )

    x_refs = (gathered, xz_send, xy_send, x_recv)
    gather_start(*x_refs)

    tile_copy.wait()
    depth = slots * GROUP
    together = n_row if n_row * n_col <= 64 else 1
    cells = together * n_col
    spread_in = (
        lax.broadcasted_iota(jnp.int32, (slots, depth), 1) // GROUP
        == lax.broadcasted_iota(jnp.int32, (slots, depth), 0)
    ).astype(BF16)
    spread_out = (
        lax.broadcasted_iota(jnp.int32, (cells * GROUP, cells), 0) // GROUP
        == lax.broadcasted_iota(jnp.int32, (cells * GROUP, cells), 1)
    ).astype(BF16)
    same_line = (
        lax.broadcasted_iota(jnp.int32, (cells * GROUP, depth), 0) % GROUP
        == lax.broadcasted_iota(jnp.int32, (cells * GROUP, depth), 1) % GROUP
    )
    cell_of = col_ids[0] * n_col + row_ids[0]
    cell_of = jnp.where(
        lax.broadcasted_iota(jnp.int32, (1, slots), 1) < live[...], cell_of, -1
    )

    def densify(step):
        cell_index = lax.broadcasted_iota(jnp.int32, (cells, slots), 0) + step * cells
        chosen = (cell_index == cell_of).astype(BF16)
        picked = dot(spread_out, dot(chosen, spread_in).astype(BF16))
        picked = jnp.where(same_line, picked, 0.0).astype(BF16)
        for pair in range(size // GROUP // 2):
            lines = [
                tiles[:, (2 * pair + h) * GROUP:(2 * pair + h + 1) * GROUP, :].reshape(depth, size)
                for h in range(2)
            ]
            block = dot(picked, jnp.concatenate(lines, axis=1)).astype(BF16)
            for c in range(together):
                for r in range(n_col):
                    at = (c * n_col + r) * GROUP
                    for h in range(2):
                        line = r * size + (2 * pair + h) * GROUP
                        adj[step * together + c, line:line + GROUP, :] = (
                            block[at:at + GROUP, h * size:(h + 1) * size]
                        )
        if pre_transpose:
            for c in range(together):
                adj_t[step * together + c] = adj[step * together + c].T

    loop(n_row // together, densify)

    rows = n_col * size
    chunk = min(rows, 512)

    def add_block(b, block, first):
        def one(step):
            at = pl.ds(step * chunk, chunk)
            product = dot(adj[b, at, :], block)
            if first:
                acc[at, :] = product
            else:
                acc[at, :] += product
        loop(rows // chunk, one)

    add_block(i, feat[...], True)
    for block_z in z_near_first:
        block = gather_pass(*x_refs, block_z)
        add_block(block, gathered[block], False)
    for block_z in (z,) + z_near_first:
        def take_features(k):
            block = gather_take(gathered, xy_send, x_recv, block_z, y_peer(k + 1))
            add_block(block, gathered[block], False)
        loop(inner - 1, take_features)

    def p_copy(to, sender):
        return send(
            part_send.at[to], part_recv.at[sender], p_send.at[to], p_recv.at[sender], "col", to
        )

    def send_partial(k):
        to = col_peer(k + 1)
        part_send[to] = acc[pl.ds(pl.multiple_of(to * size, size), size), :].astype(BF16)
        p_copy(to, j).start()

    loop(n_col - 1, send_partial)
    acc_own = pl.ds(pl.multiple_of(j * size, size), size)

    def take_partial(k):
        sender = lax.rem(j + n_col - 1 - k, n_col)
        p_copy(sender, sender).wait_recv()
        acc[acc_own, :] += part_recv[sender].astype(F32)

    loop(n_col - 1, take_partial)

    aggregate = acc[acc_own, :].astype(BF16)
    preact = dot(aggregate, weight[...]) + bias[...]
    sig = jax.nn.sigmoid(preact)
    grad_pre = (cot[...].astype(F32) * sig * (1.0 + preact * (1.0 - sig))).astype(BF16)
    grads[j] = dot(grad_pre, weight[...], ((1,), (1,))).astype(BF16)

    def g_copy(to, sender):
        return send(grads.at[j], grads.at[sender], g_send.at[to], g_recv.at[sender], "col", to)

    loop(n_col - 1, lambda k: g_copy(col_peer(k + 1), j).start())

    out[...] = (preact * sig).astype(BF16)
    local_weight = dot(aggregate, grad_pre, ((0,), (0,)))


    w_out[...] = local_weight.reshape(w_out.shape).astype(w_out.dtype)

    def w1_copy(to, sender):
        return send(w_out.at[to], w_in.at[sender], w1_send.at[to], w1_recv.at[sender], "row", to)

    loop(n_row - 1, lambda k: w1_copy(row_peer(k + 1), i).start())

    def take_grad(k):
        sender = lax.rem(j + n_col - 1 - k, n_col)
        g_copy(sender, sender).wait_recv()

    loop(n_col - 1, take_grad)

    def back(b):
        grad_rows = grads[...].reshape(rows, grads.shape[2])
        if pre_transpose:
            return dot(adj_t[b], grad_rows)
        return dot(adj[b], grad_rows, ((0,), (0,)))

    def by_copy(block_z, to, sender):
        return send(
            y_out.at[block_z * inner + to], y_in.at[block_z * inner + sender],
            by_send.at[block_z * inner + to], by_recv.at[block_z * inner + sender],
            "row", z * inner + to,
        )

    def bz_copy(to, sender):
        return send(
            z_out.at[to], z_in.at[sender], bz_send.at[to], bz_recv.at[sender],
            "row", to * inner + y,
        )

    for block_z in z_far_first + (z,):
        def send_back(k):
            to = y_peer(k + 1)
            y_out[block_z * inner + to] = back(block_z * inner + to).astype(BF16)
            by_copy(block_z, to, y).start()
        loop(inner - 1, send_back)
    for block_z in z_far_first + (z,):
        keep[block_z] = back(block_z * inner + y)

    w_sum[...] = w_out[i].astype(F32)

    def take_w1(k):
        sender = lax.rem(i + n_row - 1 - k, n_row)
        w1_copy(sender, sender).wait_recv()
        w_sum[...] += w_in[sender].astype(F32)

    loop(n_row - 1, take_w1)

    def w2_copy(to, sender):
        return send(w_sum, w_cols.at[sender], w2_send.at[to], w2_recv.at[sender], "col", to)

    loop(n_col - 1, lambda k: w2_copy(col_peer(k + 1), j).start())

    def add_back(block_z):
        def take(k):
            sender = lax.rem(y + inner - 1 - k, inner)
            by_copy(block_z, sender, sender).wait_recv()
            keep[block_z] += y_in[block_z * inner + sender].astype(F32)
        loop(inner - 1, take)

    for block_z in z_far_first:
        add_back(block_z)
        z_out[block_z] = keep[block_z].astype(BF16)
        bz_copy(block_z, z).start()

    w_cols[j] = w_sum[...]

    def take_w2(k):
        sender = lax.rem(j + n_col - 1 - k, n_col)
        w2_copy(sender, sender).wait_recv()

    loop(n_col - 1, take_w2)
    w_all[i] = jnp.sum(w_cols[...], axis=0).astype(w_all.dtype)
    w_refs = (w_all, w3z_send, w3y_send, w3_recv)
    gather_start(*w_refs)

    add_back(z)
    for block_z in z_near_first:
        gather_pass(*w_refs, block_z)
    total = keep[z]
    for block_z in z_near_first:
        bz_copy(block_z, block_z).wait_recv()
        total += z_in[block_z].astype(F32)
    grad_feat[...] = total
    for block_z in (z,) + z_near_first:
        loop(
            inner - 1,
            lambda k: gather_take(w_all, w3y_send, w3_recv, block_z, y_peer(k + 1)),
        )
    grad_w[...] = w_all[...].reshape(grad_w.shape).astype(F32)

    gather_sent(*x_refs)
    gather_sent(*w_refs)
    loop(n_row - 1, lambda k: w1_copy(row_peer(k + 1), i).wait_send())

    def col_sent(k):
        to = col_peer(k + 1)
        p_copy(to, j).wait_send()
        g_copy(to, j).wait_send()
        w2_copy(to, j).wait_send()

    loop(n_col - 1, col_sent)
    for block_z in z_near_first:
        bz_copy(block_z, z).wait_send()
    for block_z in (z,) + z_near_first:
        loop(inner - 1, lambda k: by_copy(block_z, y_peer(k + 1), y).wait_send())


def shards(n_row, n_col, features, tile_values, tile_rows, tile_cols, live_slots, weight, bias, cotangent):
    size, width = features.shape
    slots = tile_values.shape[2]
    out_width = weight.shape[1]
    rows = n_col * size
    outer = 4 if n_row % 4 == 0 else 1
    inner = n_row // outer
    pre_transpose = n_row * n_col <= 64
    strip = width // n_row
    w_kind = BF16 if strip % 16 == 0 else F32
    vmem = pl.BlockSpec(memory_space=pltpu.VMEM)
    anywhere = pl.BlockSpec(memory_space=pl.ANY)
    row_dma = pltpu.SemaphoreType.DMA((n_row,))
    col_dma = pltpu.SemaphoreType.DMA((n_col,))
    z_dma = pltpu.SemaphoreType.DMA((outer,))
    out_shape = (
        jax.ShapeDtypeStruct((size, out_width), BF16),
        jax.ShapeDtypeStruct((size, width), F32),
        jax.ShapeDtypeStruct((width, out_width), F32),
    )
    results = pl.pallas_call(
        functools.partial(kernel, n_row, n_col, outer, pre_transpose),
        out_shape=out_shape,
        in_specs=[vmem, anywhere] + [vmem] * 6,
        out_specs=(vmem, vmem, vmem),
        scratch_shapes=[
            pltpu.VMEM((slots, size, size), BF16),
            pltpu.VMEM((n_row, rows, size), BF16),
            pltpu.VMEM((n_row, size, rows) if pre_transpose else (1, 16, 128), BF16),
            pltpu.VMEM((n_row, size, width), BF16),
            pltpu.VMEM((rows, width), F32),
            pltpu.VMEM((n_col, size, width), BF16),
            pltpu.VMEM((n_col, size, width), BF16),
            pltpu.VMEM((n_col, size, width), BF16),
            pltpu.VMEM((n_row, size, width), BF16),
            pltpu.VMEM((n_row, size, width), BF16),
            pltpu.VMEM((outer, size, width), F32),
            pltpu.VMEM((outer, size, width), BF16),
            pltpu.VMEM((outer, size, width), BF16),
            pltpu.VMEM((n_row, strip, out_width), w_kind),
            pltpu.VMEM((n_row, strip, out_width), w_kind),
            pltpu.VMEM((strip, out_width), F32),
            pltpu.VMEM((n_col, strip, out_width), F32),
            pltpu.VMEM((n_row, strip, out_width), w_kind),
            pltpu.SemaphoreType.DMA,
            z_dma, row_dma, row_dma, col_dma, col_dma, col_dma, col_dma,
            row_dma, row_dma, z_dma, z_dma,
            row_dma, row_dma, col_dma, col_dma, z_dma, row_dma, row_dma,
        ],
        compiler_params=pltpu.CompilerParams(
            collective_id=0, has_side_effects=True, vmem_limit_bytes=56 * 1024 * 1024
        ),
    )(
        features, tile_values, tile_rows, tile_cols, live_slots,
        weight, bias.reshape(1, out_width), cotangent,
    )
    return results


def solution(mesh):
    return jax.shard_map(
        functools.partial(shards, mesh.shape["row"], mesh.shape["col"]),
        mesh=mesh,
        in_specs=(
            P(("col", "row"), None),
            P("row", "col", None, None, None),
            P("row", "col", None),
            P("row", "col", None),
            P("row", "col"),
            P(),
            P(),
            P(("row", "col"), None),
        ),
        out_specs=(P(("row", "col"), None), P(("col", "row"), None), P()),
        check_vma=False,
    )
```

```python
import functools

import jax
import jax.numpy as jnp
from jax import lax
from jax.experimental import pallas as pl
from jax.experimental.pallas import tpu as pltpu
from jax.sharding import PartitionSpec as P

F32 = jnp.float32
BF16 = jnp.bfloat16
GROUP = 16


def loop(count, body):
    if count <= 8:
        for step in range(count):
            body(step)
    else:
        lax.fori_loop(0, count, lambda step, carry: (body(step), carry)[1], 0)


def dot(a, b, dims=((1,), (0,))):
    return lax.dot_general(a, b, (dims, ((), ())), preferred_element_type=F32)


def kernel(
    n_row, n_col, outer, pre_transpose,
    feat_hbm, tiles_hbm, row_ids_hbm, col_ids_hbm, live, weight_hbm, bias_hbm, cot_hbm,
    out_hbm, grad_feat_hbm, grad_w_hbm,
    feat, row_ids, col_ids, weight, bias, cot, out, grad_feat, grad_w,
    tiles, adj, adj_t, gathered, acc, part_send, part_recv, grads,
    y_out, y_in, keep, z_out, z_in, w_out, w_in, w_sum, w_cols, w_all,
    load_sems, store_sems, tile_sem, xz_send, xy_send, x_recv, p_send, p_recv, g_send, g_recv,
    by_send, by_recv, bz_send, bz_recv,
    w1_send, w1_recv, w2_send, w2_recv, w3_send, w3_recv,
):
    i = lax.axis_index("row")
    j = lax.axis_index("col")
    inner = n_row // outer
    z = i // inner
    y = i % inner
    size = feat.shape[0]
    slots = tiles.shape[0]

    def row_peer(k):
        return lax.rem(i + k, n_row)

    def col_peer(k):
        return lax.rem(j + k, n_col)

    def y_peer(k):
        return lax.rem(y + k, inner)

    if outer == 4:
        near, mid, far = z + 1 - 2 * (z % 2), (z + 2) % 4, 3 - z
        within = (z % 3 + 1) // 2
        z_near_first = (near, mid + within * (far - mid), far + within * (mid - far))
        z_far_first = (mid, far, near)
    else:
        z_near_first = z_far_first = tuple((z + k) % outer for k in range(1, outer))

    def send(src, dst, send_sem, recv_sem, axis, peer):
        return pltpu.make_async_remote_copy(
            src_ref=src, dst_ref=dst, send_sem=send_sem, recv_sem=recv_sem,
            device_id={axis: peer}, device_id_type=pl.DeviceIdType.MESH,
        )

    loads = [
        pltpu.make_async_copy(src, dst, load_sems.at[k])
        for k, (src, dst) in enumerate((
            (feat_hbm, feat), (row_ids_hbm, row_ids), (col_ids_hbm, col_ids),
            (weight_hbm, weight), (bias_hbm, bias), (cot_hbm, cot),
        ))
    ]
    stores = [
        pltpu.make_async_copy(src, dst, store_sems.at[k])
        for k, (src, dst) in enumerate((
            (out, out_hbm), (grad_feat, grad_feat_hbm), (grad_w, grad_w_hbm),
        ))
    ]
    tile_copy = pltpu.make_async_copy(tiles_hbm.at[0, 0], tiles, tile_sem)
    loads[0].start()
    tile_copy.start()
    for load in loads[1:]:
        load.start()

    barrier = pltpu.get_barrier_semaphore()

    def greet_row(k):
        pl.semaphore_signal(
            barrier, inc=1, device_id={"row": row_peer(k + 1)}, device_id_type=pl.DeviceIdType.MESH
        )

    def greet_col(k):
        pl.semaphore_signal(
            barrier, inc=1, device_id={"col": col_peer(k + 1)}, device_id_type=pl.DeviceIdType.MESH
        )

    loop(n_row - 1, greet_row)
    loop(n_col - 1, greet_col)
    loads[0].wait()
    gathered[i] = feat[...]
    pl.semaphore_wait(barrier, n_row + n_col - 2)

    def along_z(buf, z_sem, recv_sem, to, block):
        return send(
            buf.at[block], buf.at[block], z_sem.at[to], recv_sem.at[block], "row", to * inner + y
        )

    def along_y(buf, y_sem, recv_sem, block_z, to, block):
        return send(
            buf.at[block], buf.at[block], y_sem.at[block_z * inner + to], recv_sem.at[block],
            "row", z * inner + to,
        )

    def gather_start(buf, z_sem, y_sem, recv_sem):
        for to in z_near_first:
            along_z(buf, z_sem, recv_sem, to, i).start()
        loop(inner - 1, lambda k: along_y(buf, y_sem, recv_sem, z, y_peer(k + 1), i).start())

    def gather_pass(buf, z_sem, y_sem, recv_sem, block_z):
        block = block_z * inner + y
        along_z(buf, z_sem, recv_sem, block_z, block).wait_recv()
        loop(
            inner - 1,
            lambda k: along_y(buf, y_sem, recv_sem, block_z, y_peer(k + 1), block).start(),
        )
        return block

    def gather_take(buf, y_sem, recv_sem, block_z, from_y):
        block = block_z * inner + from_y
        along_y(buf, y_sem, recv_sem, block_z, from_y, block).wait_recv()
        return block

    def gather_sent(buf, z_sem, y_sem, recv_sem):
        for to in z_near_first:
            along_z(buf, z_sem, recv_sem, to, i).wait_send()
        for block_z in (z,) + z_near_first:
            loop(
                inner - 1,
                lambda k: along_y(
                    buf, y_sem, recv_sem, block_z, y_peer(k + 1), block_z * inner + y
                ).wait_send(),
            )

    x_refs = (gathered, xz_send, xy_send, x_recv)
    gather_start(*x_refs)

    tile_copy.wait()
    loads[1].wait()
    loads[2].wait()
    depth = slots * GROUP
    together = n_row if n_row * n_col <= 64 else 1
    cells = together * n_col
    spread_in = (
        lax.broadcasted_iota(jnp.int32, (slots, depth), 1) // GROUP
        == lax.broadcasted_iota(jnp.int32, (slots, depth), 0)
    ).astype(BF16)
    spread_out = (
        lax.broadcasted_iota(jnp.int32, (cells * GROUP, cells), 0) // GROUP
        == lax.broadcasted_iota(jnp.int32, (cells * GROUP, cells), 1)
    ).astype(BF16)
    same_line = (
        lax.broadcasted_iota(jnp.int32, (cells * GROUP, depth), 0) % GROUP
        == lax.broadcasted_iota(jnp.int32, (cells * GROUP, depth), 1) % GROUP
    )
    cell_of = col_ids[0] * n_col + row_ids[0]
    cell_of = jnp.where(
        lax.broadcasted_iota(jnp.int32, (1, slots), 1) < live[...], cell_of, -1
    )

    def densify(step):
        cell_index = lax.broadcasted_iota(jnp.int32, (cells, slots), 0) + step * cells
        chosen = (cell_index == cell_of).astype(BF16)
        picked = dot(spread_out, dot(chosen, spread_in).astype(BF16))
        picked = jnp.where(same_line, picked, 0.0).astype(BF16)
        for pair in range(size // GROUP // 2):
            lines = [
                tiles[:, (2 * pair + h) * GROUP:(2 * pair + h + 1) * GROUP, :].reshape(depth, size)
                for h in range(2)
            ]
            block = dot(picked, jnp.concatenate(lines, axis=1)).astype(BF16)
            for c in range(together):
                for r in range(n_col):
                    at = (c * n_col + r) * GROUP
                    for h in range(2):
                        line = r * size + (2 * pair + h) * GROUP
                        adj[step * together + c, line:line + GROUP, :] = (
                            block[at:at + GROUP, h * size:(h + 1) * size]
                        )
        if pre_transpose:
            for c in range(together):
                adj_t[step * together + c] = adj[step * together + c].T

    loop(n_row // together, densify)

    rows = n_col * size
    chunk = min(rows, 512)

    def add_block(b, block, first):
        def one(step):
            at = pl.ds(step * chunk, chunk)
            product = dot(adj[b, at, :], block)
            if first:
                acc[at, :] = product
            else:
                acc[at, :] += product
        loop(rows // chunk, one)

    add_block(i, feat[...], True)
    for block_z in z_near_first:
        block = gather_pass(*x_refs, block_z)
        add_block(block, gathered[block], False)
    for block_z in (z,) + z_near_first:
        def take_features(k):
            block = gather_take(gathered, xy_send, x_recv, block_z, y_peer(k + 1))
            add_block(block, gathered[block], False)
        loop(inner - 1, take_features)

    def p_copy(to, sender):
        return send(
            part_send.at[to], part_recv.at[sender], p_send.at[to], p_recv.at[sender], "col", to
        )

    def send_partial(k):
        to = col_peer(k + 1)
        part_send[to] = acc[pl.ds(pl.multiple_of(to * size, size), size), :].astype(BF16)
        p_copy(to, j).start()

    loop(n_col - 1, send_partial)
    acc_own = pl.ds(pl.multiple_of(j * size, size), size)

    def take_partial(k):
        sender = lax.rem(j + n_col - 1 - k, n_col)
        p_copy(sender, sender).wait_recv()
        acc[acc_own, :] += part_recv[sender].astype(F32)

    loop(n_col - 1, take_partial)

    aggregate = acc[acc_own, :].astype(BF16)
    for load in loads[3:]:
        load.wait()
    preact = dot(aggregate, weight[...]) + bias[...]
    sig = jax.nn.sigmoid(preact)
    grad_pre = (cot[...].astype(F32) * sig * (1.0 + preact * (1.0 - sig))).astype(BF16)
    grads[j] = dot(grad_pre, weight[...], ((1,), (1,))).astype(BF16)

    def g_copy(to, sender):
        return send(grads.at[j], grads.at[sender], g_send.at[to], g_recv.at[sender], "col", to)

    loop(n_col - 1, lambda k: g_copy(col_peer(k + 1), j).start())

    out[...] = (preact * sig).astype(BF16)
    stores[0].start()
    local_weight = dot(aggregate, grad_pre, ((0,), (0,)))


    w_out[...] = local_weight.reshape(w_out.shape).astype(w_out.dtype)

    def w1_copy(to, sender):
        return send(w_out.at[to], w_in.at[sender], w1_send.at[to], w1_recv.at[sender], "row", to)

    loop(n_row - 1, lambda k: w1_copy(row_peer(k + 1), i).start())

    def take_grad(k):
        sender = lax.rem(j + n_col - 1 - k, n_col)
        g_copy(sender, sender).wait_recv()

    loop(n_col - 1, take_grad)

    def back(b):
        grad_rows = grads[...].reshape(rows, grads.shape[2])
        if pre_transpose:
            return dot(adj_t[b], grad_rows)
        return dot(adj[b], grad_rows, ((0,), (0,)))

    def by_copy(block_z, to, sender):
        return send(
            y_out.at[block_z * inner + to], y_in.at[block_z * inner + sender],
            by_send.at[block_z * inner + to], by_recv.at[block_z * inner + sender],
            "row", z * inner + to,
        )

    def bz_copy(to, sender):
        return send(
            z_out.at[to], z_in.at[sender], bz_send.at[to], bz_recv.at[sender],
            "row", to * inner + y,
        )

    for block_z in z_far_first + (z,):
        def send_back(k):
            to = y_peer(k + 1)
            y_out[block_z * inner + to] = back(block_z * inner + to).astype(BF16)
            by_copy(block_z, to, y).start()
        loop(inner - 1, send_back)
    for block_z in z_far_first + (z,):
        keep[block_z] = back(block_z * inner + y)

    w_sum[...] = w_out[i].astype(F32)

    def take_w1(k):
        sender = lax.rem(i + n_row - 1 - k, n_row)
        w1_copy(sender, sender).wait_recv()
        w_sum[...] += w_in[sender].astype(F32)

    loop(n_row - 1, take_w1)

    def w2_copy(to, sender):
        return send(w_sum, w_cols.at[sender], w2_send.at[to], w2_recv.at[sender], "col", to)

    loop(n_col - 1, lambda k: w2_copy(col_peer(k + 1), j).start())

    def add_back(block_z):
        def take(k):
            sender = lax.rem(y + inner - 1 - k, inner)
            by_copy(block_z, sender, sender).wait_recv()
            keep[block_z] += y_in[block_z * inner + sender].astype(F32)
        loop(inner - 1, take)

    def pass_back(block_z):
        add_back(block_z)
        z_out[block_z] = keep[block_z].astype(BF16)
        bz_copy(block_z, z).start()

    for block_z in z_far_first[:2]:
        pass_back(block_z)

    w_cols[j] = w_sum[...]

    def take_w2(k):
        sender = lax.rem(j + n_col - 1 - k, n_col)
        w2_copy(sender, sender).wait_recv()

    loop(n_col - 1, take_w2)
    w_all[i] = jnp.sum(w_cols[...], axis=0).astype(w_all.dtype)

    def w3_copy(to, sender):
        return send(
            w_all.at[sender], w_all.at[sender], w3_send.at[to], w3_recv.at[sender], "row", to
        )

    loop(n_row - 1, lambda k: w3_copy(row_peer(k + 1), i).start())

    for block_z in z_far_first[2:]:
        pass_back(block_z)
    add_back(z)
    total = keep[z]
    for block_z in z_near_first:
        bz_copy(block_z, block_z).wait_recv()
        total += z_in[block_z].astype(F32)
    grad_feat[...] = total
    stores[1].start()

    def take_w3(k):
        sender = lax.rem(i + n_row - 1 - k, n_row)
        w3_copy(sender, sender).wait_recv()

    loop(n_row - 1, take_w3)
    grad_w[...] = w_all[...].reshape(grad_w.shape).astype(F32)
    stores[2].start()

    gather_sent(*x_refs)
    loop(n_row - 1, lambda k: w1_copy(row_peer(k + 1), i).wait_send())
    loop(n_row - 1, lambda k: w3_copy(row_peer(k + 1), i).wait_send())

    def col_sent(k):
        to = col_peer(k + 1)
        p_copy(to, j).wait_send()
        g_copy(to, j).wait_send()
        w2_copy(to, j).wait_send()

    loop(n_col - 1, col_sent)
    for block_z in z_near_first:
        bz_copy(block_z, z).wait_send()
    for block_z in (z,) + z_near_first:
        loop(inner - 1, lambda k: by_copy(block_z, y_peer(k + 1), y).wait_send())
    for store in stores:
        store.wait()


def hand_over(*refs):
    sources, results, held = refs[:3], refs[3:6], refs[6:9]
    sems = refs[9]
    loads = [pltpu.make_async_copy(sources[k], held[k], sems.at[k]) for k in range(3)]
    stores = [pltpu.make_async_copy(held[k], results[k], sems.at[3 + k]) for k in range(3)]
    for load in loads:
        load.start()
    for load, store in zip(loads, stores):
        load.wait()
        store.start()
    for store in stores:
        store.wait()


def shards(n_row, n_col, features, tile_values, tile_rows, tile_cols, live_slots, weight, bias, cotangent):
    size, width = features.shape
    slots = tile_values.shape[2]
    out_width = weight.shape[1]
    rows = n_col * size
    outer = 4 if n_row % 4 == 0 else 1
    inner = n_row // outer
    pre_transpose = n_row * n_col <= 64
    strip = width // n_row
    w_kind = BF16 if strip % 16 == 0 else F32
    vmem = pl.BlockSpec(memory_space=pltpu.VMEM)
    anywhere = pl.BlockSpec(memory_space=pl.ANY)
    row_dma = pltpu.SemaphoreType.DMA((n_row,))
    col_dma = pltpu.SemaphoreType.DMA((n_col,))
    z_dma = pltpu.SemaphoreType.DMA((outer,))
    out_shape = (
        jax.ShapeDtypeStruct((size, out_width), BF16),
        jax.ShapeDtypeStruct((size, width), F32),
        jax.ShapeDtypeStruct((width, out_width), F32),
    )
    results = pl.pallas_call(
        functools.partial(kernel, n_row, n_col, outer, pre_transpose),
        out_shape=out_shape,
        in_specs=[anywhere] * 4 + [vmem] + [anywhere] * 3,
        out_specs=(anywhere,) * 3,
        scratch_shapes=[
            pltpu.VMEM((size, width), BF16),
            pltpu.VMEM((1, 1, slots), jnp.int32),
            pltpu.VMEM((1, 1, slots), jnp.int32),
            pltpu.VMEM((width, out_width), BF16),
            pltpu.VMEM((1, out_width), F32),
            pltpu.VMEM((size, out_width), BF16),
            pltpu.VMEM((size, out_width), BF16),
            pltpu.VMEM((size, width), F32),
            pltpu.VMEM((width, out_width), F32),
            pltpu.VMEM((slots, size, size), BF16),
            pltpu.VMEM((n_row, rows, size), BF16),
            pltpu.VMEM((n_row, size, rows) if pre_transpose else (1, 16, 128), BF16),
            pltpu.VMEM((n_row, size, width), BF16),
            pltpu.VMEM((rows, width), F32),
            pltpu.VMEM((n_col, size, width), BF16),
            pltpu.VMEM((n_col, size, width), BF16),
            pltpu.VMEM((n_col, size, width), BF16),
            pltpu.VMEM((n_row, size, width), BF16),
            pltpu.VMEM((n_row, size, width), BF16),
            pltpu.VMEM((outer, size, width), F32),
            pltpu.VMEM((outer, size, width), BF16),
            pltpu.VMEM((outer, size, width), BF16),
            pltpu.VMEM((n_row, strip, out_width), w_kind),
            pltpu.VMEM((n_row, strip, out_width), w_kind),
            pltpu.VMEM((strip, out_width), F32),
            pltpu.VMEM((n_col, strip, out_width), F32),
            pltpu.VMEM((n_row, strip, out_width), w_kind),
            pltpu.SemaphoreType.DMA((6,)),
            pltpu.SemaphoreType.DMA((3,)),
            pltpu.SemaphoreType.DMA,
            z_dma, row_dma, row_dma, col_dma, col_dma, col_dma, col_dma,
            row_dma, row_dma, z_dma, z_dma,
            row_dma, row_dma, col_dma, col_dma, row_dma, row_dma,
        ],
        compiler_params=pltpu.CompilerParams(
            collective_id=0, has_side_effects=True, vmem_limit_bytes=56 * 1024 * 1024
        ),
    )(
        features, tile_values, tile_rows, tile_cols, live_slots,
        weight, bias.reshape(1, out_width), cotangent,
    )
    return pl.pallas_call(
        hand_over,
        out_shape=out_shape,
        in_specs=[anywhere] * 3,
        out_specs=(anywhere,) * 3,
        scratch_shapes=[pltpu.VMEM(a.shape, a.dtype) for a in out_shape]
        + [pltpu.SemaphoreType.DMA((6,))],
    )(*results)


def solution(mesh):
    return jax.shard_map(
        functools.partial(shards, mesh.shape["row"], mesh.shape["col"]),
        mesh=mesh,
        in_specs=(
            P(("col", "row"), None),
            P("row", "col", None, None, None),
            P("row", "col", None),
            P("row", "col", None),
            P("row", "col"),
            P(),
            P(),
            P(("row", "col"), None),
        ),
        out_specs=(P(("row", "col"), None), P(("col", "row"), None), P()),
        check_vma=False,
    )
```

```python
import functools

import jax
import jax.numpy as jnp
from jax import lax
from jax.experimental import pallas as pl
from jax.experimental.pallas import tpu as pltpu
from jax.sharding import PartitionSpec as P

F32 = jnp.float32
BF16 = jnp.bfloat16
GROUP = 16


def loop(count, body):
    if count <= 8:
        for step in range(count):
            body(step)
    else:
        lax.fori_loop(0, count, lambda step, carry: (body(step), carry)[1], 0)


def dot(a, b, dims=((1,), (0,))):
    return lax.dot_general(a, b, (dims, ((), ())), preferred_element_type=F32)


def kernel(
    n_row, n_col, outer, pre_transpose,
    feat_hbm, tiles_hbm, row_ids_hbm, col_ids_hbm, live, weight_hbm, bias_hbm, cot_hbm,
    out_hbm, grad_feat_hbm, grad_w_hbm,
    feat, row_ids, col_ids, weight, bias, cot, out, grad_feat, grad_w,
    tiles, adj, adj_t, gathered, acc, chip_in, part_send, part_recv, grads,
    y_out, y_in, keep, z_out, z_in, w_out, w_in, w_sum, w_cols, w_all,
    load_sems, store_sems, tile_sem, xz_send, xy_send, x_recv, p1_send, p1_recv, p_send, p_recv, g_send, g1_send, g_recv,
    by_send, by_recv, bz_send, bz_recv,
    w1_send, w1_recv, w2_send, w2_recv, w3_send, w3_recv,
):
    i = lax.axis_index("row")
    j = lax.axis_index("col")
    inner = n_row // outer
    z = i // inner
    y = i % inner
    size = feat.shape[0]
    slots = tiles.shape[0]

    def row_peer(k):
        return lax.rem(i + k, n_row)

    def col_peer(k):
        return lax.rem(j + k, n_col)

    pairs = n_col // 2
    pair = j // 2
    core = j % 2
    partner = 2 * pair + 1 - core

    def pair_peer(k):
        return lax.rem(pair + k, pairs)

    def y_peer(k):
        return lax.rem(y + k, inner)

    if outer == 4:
        near, mid, far = z + 1 - 2 * (z % 2), (z + 2) % 4, 3 - z
        within = (z % 3 + 1) // 2
        z_near_first = (near, mid + within * (far - mid), far + within * (mid - far))
        z_far_first = (mid, far, near)
    else:
        z_near_first = z_far_first = tuple((z + k) % outer for k in range(1, outer))

    def send(src, dst, send_sem, recv_sem, axis, peer):
        return pltpu.make_async_remote_copy(
            src_ref=src, dst_ref=dst, send_sem=send_sem, recv_sem=recv_sem,
            device_id={axis: peer}, device_id_type=pl.DeviceIdType.MESH,
        )

    loads = [
        pltpu.make_async_copy(src, dst, load_sems.at[k])
        for k, (src, dst) in enumerate((
            (feat_hbm, feat), (row_ids_hbm, row_ids), (col_ids_hbm, col_ids),
            (weight_hbm, weight), (bias_hbm, bias), (cot_hbm, cot),
        ))
    ]
    stores = [
        pltpu.make_async_copy(src, dst, store_sems.at[k])
        for k, (src, dst) in enumerate((
            (out, out_hbm), (grad_feat, grad_feat_hbm), (grad_w, grad_w_hbm),
        ))
    ]
    tile_copy = pltpu.make_async_copy(tiles_hbm.at[0, 0], tiles, tile_sem)
    loads[0].start()
    tile_copy.start()
    for load in loads[1:]:
        load.start()

    barrier = pltpu.get_barrier_semaphore()

    def greet_row(k):
        pl.semaphore_signal(
            barrier, inc=1, device_id={"row": row_peer(k + 1)}, device_id_type=pl.DeviceIdType.MESH
        )

    def greet_col(k):
        pl.semaphore_signal(
            barrier, inc=1, device_id={"col": col_peer(k + 1)}, device_id_type=pl.DeviceIdType.MESH
        )

    loop(n_row - 1, greet_row)
    loop(n_col - 1, greet_col)
    loads[0].wait()
    gathered[i] = feat[...]
    pl.semaphore_wait(barrier, n_row + n_col - 2)

    def along_z(buf, z_sem, recv_sem, to, block):
        return send(
            buf.at[block], buf.at[block], z_sem.at[to], recv_sem.at[block], "row", to * inner + y
        )

    def along_y(buf, y_sem, recv_sem, block_z, to, block):
        return send(
            buf.at[block], buf.at[block], y_sem.at[block_z * inner + to], recv_sem.at[block],
            "row", z * inner + to,
        )

    def gather_start(buf, z_sem, y_sem, recv_sem):
        for to in z_near_first:
            along_z(buf, z_sem, recv_sem, to, i).start()
        loop(inner - 1, lambda k: along_y(buf, y_sem, recv_sem, z, y_peer(k + 1), i).start())

    def gather_pass(buf, z_sem, y_sem, recv_sem, block_z):
        block = block_z * inner + y
        along_z(buf, z_sem, recv_sem, block_z, block).wait_recv()
        loop(
            inner - 1,
            lambda k: along_y(buf, y_sem, recv_sem, block_z, y_peer(k + 1), block).start(),
        )
        return block

    def gather_take(buf, y_sem, recv_sem, block_z, from_y):
        block = block_z * inner + from_y
        along_y(buf, y_sem, recv_sem, block_z, from_y, block).wait_recv()
        return block

    def gather_sent(buf, z_sem, y_sem, recv_sem):
        for to in z_near_first:
            along_z(buf, z_sem, recv_sem, to, i).wait_send()
        for block_z in (z,) + z_near_first:
            loop(
                inner - 1,
                lambda k: along_y(
                    buf, y_sem, recv_sem, block_z, y_peer(k + 1), block_z * inner + y
                ).wait_send(),
            )

    x_refs = (gathered, xz_send, xy_send, x_recv)
    gather_start(*x_refs)

    tile_copy.wait()
    loads[1].wait()
    loads[2].wait()
    depth = slots * GROUP
    together = n_row if n_row * n_col <= 64 else 1
    cells = together * n_col
    spread_in = (
        lax.broadcasted_iota(jnp.int32, (slots, depth), 1) // GROUP
        == lax.broadcasted_iota(jnp.int32, (slots, depth), 0)
    ).astype(BF16)
    spread_out = (
        lax.broadcasted_iota(jnp.int32, (cells * GROUP, cells), 0) // GROUP
        == lax.broadcasted_iota(jnp.int32, (cells * GROUP, cells), 1)
    ).astype(BF16)
    same_line = (
        lax.broadcasted_iota(jnp.int32, (cells * GROUP, depth), 0) % GROUP
        == lax.broadcasted_iota(jnp.int32, (cells * GROUP, depth), 1) % GROUP
    )
    cell_of = col_ids[0] * n_col + row_ids[0]
    cell_of = jnp.where(
        lax.broadcasted_iota(jnp.int32, (1, slots), 1) < live[...], cell_of, -1
    )

    def densify(step):
        cell_index = lax.broadcasted_iota(jnp.int32, (cells, slots), 0) + step * cells
        chosen = (cell_index == cell_of).astype(BF16)
        picked = dot(spread_out, dot(chosen, spread_in).astype(BF16))
        picked = jnp.where(same_line, picked, 0.0).astype(BF16)
        for pair in range(size // GROUP // 2):
            lines = [
                tiles[:, (2 * pair + h) * GROUP:(2 * pair + h + 1) * GROUP, :].reshape(depth, size)
                for h in range(2)
            ]
            block = dot(picked, jnp.concatenate(lines, axis=1)).astype(BF16)
            for c in range(together):
                for r in range(n_col):
                    at = (c * n_col + r) * GROUP
                    for h in range(2):
                        line = r * size + (2 * pair + h) * GROUP
                        adj[step * together + c, line:line + GROUP, :] = (
                            block[at:at + GROUP, h * size:(h + 1) * size]
                        )
        if pre_transpose:
            for c in range(together):
                adj_t[step * together + c] = adj[step * together + c].T

    loop(n_row // together, densify)

    rows = n_col * size
    chunk = min(rows, 512)

    def add_block(b, block, first):
        def one(step):
            at = pl.ds(step * chunk, chunk)
            product = dot(adj[b, at, :], block)
            if first:
                acc[at, :] = product
            else:
                acc[at, :] += product
        loop(rows // chunk, one)

    add_block(i, feat[...], True)
    for block_z in z_near_first:
        block = gather_pass(*x_refs, block_z)
        add_block(block, gathered[block], False)
    for block_z in (z,) + z_near_first:
        def take_features(k):
            block = gather_take(gathered, xy_send, x_recv, block_z, y_peer(k + 1))
            add_block(block, gathered[block], False)
        loop(inner - 1, take_features)

    def p1_copy(pair):
        to = 2 * pair + 1 - core
        return send(
            acc.at[pl.ds(pl.multiple_of(to * size, size), size), :], chip_in.at[pair],
            p1_send.at[pair], p1_recv.at[pair], "col", partner,
        )

    def p_copy(to, sender):
        return send(
            part_send.at[to], part_recv.at[sender], p_send.at[to], p_recv.at[sender],
            "col", 2 * to + core,
        )

    def mine(pair):
        return pl.ds(pl.multiple_of((2 * pair + core) * size, size), size)

    loop(pairs, lambda k: p1_copy(pair_peer(k + 1)).start())

    def send_partial(k):
        to = pair_peer(k + 1)
        p1_copy(to).wait_recv()
        part_send[to] = (acc[mine(to), :] + chip_in[to]).astype(BF16)
        p_copy(to, pair).start()

    loop(pairs - 1, send_partial)
    p1_copy(pair).wait_recv()
    acc_own = mine(pair)
    acc[acc_own, :] += chip_in[pair]

    def take_partial(k):
        sender = pair_peer(pairs - 1 - k)
        p_copy(sender, sender).wait_recv()
        acc[acc_own, :] += part_recv[sender].astype(F32)

    loop(pairs - 1, take_partial)

    aggregate = acc[acc_own, :].astype(BF16)
    for load in loads[3:]:
        load.wait()
    preact = dot(aggregate, weight[...]) + bias[...]
    sig = jax.nn.sigmoid(preact)
    grad_pre = (cot[...].astype(F32) * sig * (1.0 + preact * (1.0 - sig))).astype(BF16)
    grads[j] = dot(grad_pre, weight[...], ((1,), (1,))).astype(BF16)

    def g_copy(to, sender):
        return send(grads.at[j], grads.at[sender], g_send.at[to], g_recv.at[sender], "col", to)

    loop(n_col - 1, lambda k: g_copy(col_peer(k + 1), j).start())

    out[...] = (preact * sig).astype(BF16)
    stores[0].start()
    local_weight = dot(aggregate, grad_pre, ((0,), (0,)))


    w_out[...] = local_weight.reshape(w_out.shape).astype(w_out.dtype)

    def w1_copy(to, sender):
        return send(w_out.at[to], w_in.at[sender], w1_send.at[to], w1_recv.at[sender], "row", to)

    loop(n_row - 1, lambda k: w1_copy(row_peer(k + 1), i).start())

    def take_grad(k):
        sender = lax.rem(j + n_col - 1 - k, n_col)
        g_copy(sender, sender).wait_recv()

    loop(n_col - 1, take_grad)

    def back(b):
        grad_rows = grads[...].reshape(rows, grads.shape[2])
        if pre_transpose:
            return dot(adj_t[b], grad_rows)
        return dot(adj[b], grad_rows, ((0,), (0,)))

    def by_copy(block_z, to, sender):
        return send(
            y_out.at[block_z * inner + to], y_in.at[block_z * inner + sender],
            by_send.at[block_z * inner + to], by_recv.at[block_z * inner + sender],
            "row", z * inner + to,
        )

    def bz_copy(to, sender):
        return send(
            z_out.at[to], z_in.at[sender], bz_send.at[to], bz_recv.at[sender],
            "row", to * inner + y,
        )

    for block_z in z_far_first + (z,):
        def send_back(k):
            to = y_peer(k + 1)
            y_out[block_z * inner + to] = back(block_z * inner + to).astype(BF16)
            by_copy(block_z, to, y).start()
        loop(inner - 1, send_back)
    for block_z in z_far_first + (z,):
        keep[block_z] = back(block_z * inner + y)

    w_sum[...] = w_out[i].astype(F32)

    def take_w1(k):
        sender = lax.rem(i + n_row - 1 - k, n_row)
        w1_copy(sender, sender).wait_recv()
        w_sum[...] += w_in[sender].astype(F32)

    loop(n_row - 1, take_w1)

    def w2_copy(to, sender):
        return send(w_sum, w_cols.at[sender], w2_send.at[to], w2_recv.at[sender], "col", to)

    loop(n_col - 1, lambda k: w2_copy(col_peer(k + 1), j).start())

    def add_back(block_z):
        def take(k):
            sender = lax.rem(y + inner - 1 - k, inner)
            by_copy(block_z, sender, sender).wait_recv()
            keep[block_z] += y_in[block_z * inner + sender].astype(F32)
        loop(inner - 1, take)

    def pass_back(block_z):
        add_back(block_z)
        z_out[block_z] = keep[block_z].astype(BF16)
        bz_copy(block_z, z).start()

    for block_z in z_far_first:
        pass_back(block_z)

    w_cols[j] = w_sum[...]

    def take_w2(k):
        sender = lax.rem(j + n_col - 1 - k, n_col)
        w2_copy(sender, sender).wait_recv()

    loop(n_col - 1, take_w2)
    w_all[i] = jnp.sum(w_cols[...], axis=0).astype(w_all.dtype)

    def w3_copy(to, sender):
        return send(
            w_all.at[sender], w_all.at[sender], w3_send.at[to], w3_recv.at[sender], "row", to
        )

    loop(n_row - 1, lambda k: w3_copy(row_peer(k + 1), i).start())

    add_back(z)
    total = keep[z]
    for block_z in z_near_first:
        bz_copy(block_z, block_z).wait_recv()
        total += z_in[block_z].astype(F32)
    grad_feat[...] = total
    stores[1].start()

    def take_w3(k):
        sender = lax.rem(i + n_row - 1 - k, n_row)
        w3_copy(sender, sender).wait_recv()

    loop(n_row - 1, take_w3)
    grad_w[...] = w_all[...].reshape(grad_w.shape).astype(F32)
    stores[2].start()

    gather_sent(*x_refs)
    loop(n_row - 1, lambda k: w1_copy(row_peer(k + 1), i).wait_send())
    loop(n_row - 1, lambda k: w3_copy(row_peer(k + 1), i).wait_send())

    def col_sent(k):
        to = col_peer(k + 1)
        w2_copy(to, j).wait_send()
        g_copy(to, j).wait_send()

    loop(n_col - 1, col_sent)

    def pair_sent(k):
        to = pair_peer(k + 1)
        p_copy(to, pair).wait_send()

    def chip_sent(k):
        p1_copy(k).wait_send()

    loop(pairs - 1, pair_sent)
    loop(pairs, chip_sent)
    for block_z in z_near_first:
        bz_copy(block_z, z).wait_send()
    for block_z in (z,) + z_near_first:
        loop(inner - 1, lambda k: by_copy(block_z, y_peer(k + 1), y).wait_send())
    for store in stores:
        store.wait()


def hand_over(*refs):
    sources, results, held = refs[:3], refs[3:6], refs[6:9]
    sems = refs[9]
    loads = [pltpu.make_async_copy(sources[k], held[k], sems.at[k]) for k in range(3)]
    stores = [pltpu.make_async_copy(held[k], results[k], sems.at[3 + k]) for k in range(3)]
    for load in loads:
        load.start()
    for load, store in zip(loads, stores):
        load.wait()
        store.start()
    for store in stores:
        store.wait()


def shards(n_row, n_col, features, tile_values, tile_rows, tile_cols, live_slots, weight, bias, cotangent):
    size, width = features.shape
    slots = tile_values.shape[2]
    out_width = weight.shape[1]
    rows = n_col * size
    outer = 4 if n_row % 4 == 0 else 1
    inner = n_row // outer
    pre_transpose = n_row * n_col <= 64
    strip = width // n_row
    w_kind = BF16 if strip % 16 == 0 else F32
    vmem = pl.BlockSpec(memory_space=pltpu.VMEM)
    anywhere = pl.BlockSpec(memory_space=pl.ANY)
    row_dma = pltpu.SemaphoreType.DMA((n_row,))
    col_dma = pltpu.SemaphoreType.DMA((n_col,))
    pair_dma = pltpu.SemaphoreType.DMA((n_col // 2,))
    z_dma = pltpu.SemaphoreType.DMA((outer,))
    out_shape = (
        jax.ShapeDtypeStruct((size, out_width), BF16),
        jax.ShapeDtypeStruct((size, width), F32),
        jax.ShapeDtypeStruct((width, out_width), F32),
    )
    results = pl.pallas_call(
        functools.partial(kernel, n_row, n_col, outer, pre_transpose),
        out_shape=out_shape,
        in_specs=[anywhere] * 4 + [vmem] + [anywhere] * 3,
        out_specs=(anywhere,) * 3,
        scratch_shapes=[
            pltpu.VMEM((size, width), BF16),
            pltpu.VMEM((1, 1, slots), jnp.int32),
            pltpu.VMEM((1, 1, slots), jnp.int32),
            pltpu.VMEM((width, out_width), BF16),
            pltpu.VMEM((1, out_width), F32),
            pltpu.VMEM((size, out_width), BF16),
            pltpu.VMEM((size, out_width), BF16),
            pltpu.VMEM((size, width), F32),
            pltpu.VMEM((width, out_width), F32),
            pltpu.VMEM((slots, size, size), BF16),
            pltpu.VMEM((n_row, rows, size), BF16),
            pltpu.VMEM((n_row, size, rows) if pre_transpose else (1, 16, 128), BF16),
            pltpu.VMEM((n_row, size, width), BF16),
            pltpu.VMEM((rows, width), F32),
            pltpu.VMEM((n_col // 2, size, width), F32),
            pltpu.VMEM((n_col // 2, size, width), BF16),
            pltpu.VMEM((n_col // 2, size, width), BF16),
            pltpu.VMEM((n_col, size, width), BF16),
            pltpu.VMEM((n_row, size, width), BF16),
            pltpu.VMEM((n_row, size, width), BF16),
            pltpu.VMEM((outer, size, width), F32),
            pltpu.VMEM((outer, size, width), BF16),
            pltpu.VMEM((outer, size, width), BF16),
            pltpu.VMEM((n_row, strip, out_width), w_kind),
            pltpu.VMEM((n_row, strip, out_width), w_kind),
            pltpu.VMEM((strip, out_width), F32),
            pltpu.VMEM((n_col, strip, out_width), F32),
            pltpu.VMEM((n_row, strip, out_width), w_kind),
            pltpu.SemaphoreType.DMA((6,)),
            pltpu.SemaphoreType.DMA((3,)),
            pltpu.SemaphoreType.DMA,
            z_dma, row_dma, row_dma, pair_dma, pair_dma, pair_dma, pair_dma,
            col_dma, pair_dma, col_dma,
            row_dma, row_dma, z_dma, z_dma,
            row_dma, row_dma, col_dma, col_dma, row_dma, row_dma,
        ],
        compiler_params=pltpu.CompilerParams(
            collective_id=0, has_side_effects=True, vmem_limit_bytes=56 * 1024 * 1024
        ),
    )(
        features, tile_values, tile_rows, tile_cols, live_slots,
        weight, bias.reshape(1, out_width), cotangent,
    )
    return pl.pallas_call(
        hand_over,
        out_shape=out_shape,
        in_specs=[anywhere] * 3,
        out_specs=(anywhere,) * 3,
        scratch_shapes=[pltpu.VMEM(a.shape, a.dtype) for a in out_shape]
        + [pltpu.SemaphoreType.DMA((6,))],
    )(*results)


def solution(mesh):
    return jax.shard_map(
        functools.partial(shards, mesh.shape["row"], mesh.shape["col"]),
        mesh=mesh,
        in_specs=(
            P(("col", "row"), None),
            P("row", "col", None, None, None),
            P("row", "col", None),
            P("row", "col", None),
            P("row", "col"),
            P(),
            P(),
            P(("row", "col"), None),
        ),
        out_specs=(P(("row", "col"), None), P(("col", "row"), None), P()),
        check_vma=False,
    )
```
